32 devices in a mesh: seq: 16 (over z, x, core), tp: 2 (over y).
Axes of the slice: x: 2, y: 2, z: 4, core: 2. Of those that a mesh axis runs over, the one named last changes fastest.
Arguments:
- residual: bfloat16 [4096, 5376], P('seq', 'tp'), may hold values from -10.5 to 10.5
- input_gain: float32 [5376], replicated, may hold values from 0.25 to 1.75
- w_query: bfloat16 [5376, 4096], P('seq', 'tp'), may hold values from -0.078125 to 0.078125
- key_weight: bfloat16 [5376, 2048], P('seq', 'tp'), may hold values from -0.078125 to 0.078125
- value_weight: bfloat16 [5376, 2048], P('seq', 'tp'), may hold values from -0.078125 to 0.078125
- query_gain: float32 [128], replicated, may hold values from 0.25 to 1.75
- key_gain: float32 [128], replicated, may hold values from 0.25 to 1.75
- w_out: bfloat16 [4096, 5376], P('tp', 'seq'), may hold values from -0.1640625 to 0.1640625
- post_gain: float32 [5376], replicated, may hold values from 0.25 to 1.75
- positions: int32 [4096], replicated, may hold values from 0 to 5631, as said below
Outputs:
- mixed: bfloat16 [4096, 5376], P('seq', 'tp')
The draws below stay inside these ranges and needn't reach their ends.
Inputs may be any that keep to these rules, and one draw needn't show every extreme that they name: positions start at 0 and rise by 1 over the first 1024 tokens; after that they rise by 1 or 2 from each token to the next, by 2 at exactly (3072) // 2 tokens.
All inputs are finite; a program needn't handle non-finite values.
Results may differ from the reference program's by a relative error of at most 0.017.
Values may be sent and summed in bfloat16 or wider, within the bound.
A program may use at most 128 MiB of HBM per device.

```python
import jax
import jax.numpy as jnp
from jax import lax

MODEL_WIDTH = 5376
QUERY_HEADS = 32
KEY_VALUE_HEADS = 16
HEAD_SIZE = 128
LOOKBACK_SPAN = 1024
T_SEQ = 256
DOCUMENT_TOKENS = 4096
N_TP = 2


def column_profile(key, width):
    rise_log = 1.1
    places = jnp.arange(width, dtype=jnp.float32) / width - 0.5
    jitter = jax.random.uniform(key, (width,), jnp.float32, -0.35, 0.35)
    return jnp.exp(rise_log * places + jitter)


def draw_residual(key, part):
    first_key, second_key = jax.random.split(key, 2)
    profile = column_profile(first_key, MODEL_WIDTH)
    value_matrix = jnp.clip(jax.random.normal(second_key, (DOCUMENT_TOKENS, MODEL_WIDTH), jnp.float32), -4.0, 4.0) * profile
    return value_matrix.astype(jnp.bfloat16)


def draw_w_out(key, part):
    first_key, second_key = jax.random.split(key)
    profile = column_profile(first_key, MODEL_WIDTH)
    fan_scale = (QUERY_HEADS * HEAD_SIZE) ** (-0.5)
    base = jnp.clip(jax.random.normal(second_key, (QUERY_HEADS * HEAD_SIZE, MODEL_WIDTH), jnp.float32), -4.0, 4.0)
    return (base * fan_scale * profile).astype(jnp.bfloat16)


def draw_positions(key, part):
    later = DOCUMENT_TOKENS - LOOKBACK_SPAN
    doubled = later // 2
    order = jax.random.permutation(key, later)
    twos = jnp.zeros((later,), jnp.int32).at[order[:doubled]].set(1)
    steps = jnp.concatenate([jnp.zeros((1,), jnp.int32), jnp.ones((LOOKBACK_SPAN - 1,), jnp.int32), 1 + twos])
    return jnp.cumsum(steps).astype(jnp.int32)


def block_scale(stream_key, dims, shards, low, high):
    loudness = 1.0
    for position, parts in shards:
        heights = jax.random.uniform(jax.random.fold_in(jax.random.fold_in(stream_key, 6), position), (parts,), jnp.float32, low / len(shards), high / len(shards))
        loudness = loudness * jnp.repeat(jnp.exp(heights), dims[position] // parts).reshape((-1,) + (1,) * (len(dims) - 1 - position))
    return loudness


def bell_draw(key, dims, scale, reach, cuts=(), kind=jnp.bfloat16):
    level = block_scale(key, dims, cuts, -0.22, 0.18) if cuts else 1.0
    entries = jax.random.normal(key, dims, jnp.float32) * scale * level
    return jnp.minimum(jnp.maximum(entries, -reach), reach).astype(kind)


def setup_inputs(seed: int = 0) -> dict:
    arg_keys = jax.random.split(jax.random.key(seed), 11)
    return {
        "residual": draw_residual(jax.random.fold_in(arg_keys[10], 71), 0),
        "input_gain": jnp.clip(1.0 + 0.15 * jax.random.normal(arg_keys[1], (MODEL_WIDTH,), jnp.float32), 0.25, 1.75),
        "w_query": bell_draw(arg_keys[2], (MODEL_WIDTH, QUERY_HEADS * HEAD_SIZE), MODEL_WIDTH ** -0.5, 0.078125, ((0, 16), (1, 2))),
        "key_weight": bell_draw(arg_keys[3], (MODEL_WIDTH, KEY_VALUE_HEADS * HEAD_SIZE), MODEL_WIDTH ** -0.5, 0.078125, ((0, 16), (1, 2))),
        "value_weight": bell_draw(arg_keys[4], (MODEL_WIDTH, KEY_VALUE_HEADS * HEAD_SIZE), MODEL_WIDTH ** -0.5, 0.078125, ((0, 16), (1, 2))),
        "query_gain": jnp.clip(1.0 + 0.15 * jax.random.normal(arg_keys[5], (HEAD_SIZE,), jnp.float32), 0.25, 1.75),
        "key_gain": jnp.clip(1.0 + 0.15 * jax.random.normal(arg_keys[6], (HEAD_SIZE,), jnp.float32), 0.25, 1.75),
        "w_out": draw_w_out(jax.random.fold_in(arg_keys[10], 71), 0),
        "post_gain": jnp.clip(1.0 + 0.15 * jax.random.normal(arg_keys[8], (MODEL_WIDTH,), jnp.float32), 0.25, 1.75),
        "positions": draw_positions(jax.random.fold_in(arg_keys[10], 71), 0),
    }


epsilon = 1e-06
score_scale = 168.0 ** (-0.5)
rotary_base = 10000.0

def norm_scale(value_matrix, gain):
    mean_square = lax.optimization_barrier(jnp.mean(value_matrix * value_matrix, axis=-1, keepdims=True))
    return value_matrix * lax.rsqrt(mean_square + epsilon) * gain

def rotary(value_matrix, places):
    half_dim = value_matrix.shape[-1] // 2
    inverse = rotary_base ** (-jnp.arange(half_dim, dtype=jnp.float32) / half_dim)
    angles = places.astype(jnp.float32)[:, None] * inverse[None, :]
    cosine = jnp.cos(angles)[:, None, :]
    sine = jnp.sin(angles)[:, None, :]
    first = value_matrix[..., :half_dim]
    second = value_matrix[..., half_dim:]
    return jnp.concatenate([first * cosine - second * sine, second * cosine + first * sine], axis=-1)

def reference(residual, input_gain, w_query, key_weight, value_weight, query_gain, key_gain, w_out, post_gain, positions):
    stream = residual.astype(jnp.float32)
    normalized_input = norm_scale(stream, input_gain).astype(jnp.bfloat16)
    query_group = QUERY_HEADS // KEY_VALUE_HEADS
    queries_raw = jnp.dot(normalized_input, w_query, preferred_element_type=jnp.float32).reshape(DOCUMENT_TOKENS, QUERY_HEADS, HEAD_SIZE)
    unrotated_keys = jnp.dot(normalized_input, key_weight, preferred_element_type=jnp.float32).reshape(DOCUMENT_TOKENS, KEY_VALUE_HEADS, HEAD_SIZE)
    projected_values = jnp.dot(normalized_input, value_weight, preferred_element_type=jnp.float32)
    query_matrix = rotary(norm_scale(queries_raw, query_gain), positions).astype(jnp.bfloat16)
    query_matrix = lax.optimization_barrier(query_matrix).reshape(DOCUMENT_TOKENS, KEY_VALUE_HEADS, query_group, HEAD_SIZE)
    key_matrix = lax.optimization_barrier(rotary(norm_scale(unrotated_keys, key_gain), positions).astype(jnp.bfloat16))
    value_matrix = lax.optimization_barrier(projected_values.astype(jnp.bfloat16)).reshape(DOCUMENT_TOKENS, KEY_VALUE_HEADS, HEAD_SIZE)
    padded_keys = jnp.concatenate([jnp.zeros((LOOKBACK_SPAN, KEY_VALUE_HEADS, HEAD_SIZE), jnp.bfloat16), key_matrix], axis=0)
    padded_values = jnp.concatenate([jnp.zeros((LOOKBACK_SPAN, KEY_VALUE_HEADS, HEAD_SIZE), jnp.bfloat16), value_matrix], axis=0)
    pad_places = jnp.concatenate([jnp.zeros((LOOKBACK_SPAN,), jnp.int32), positions.astype(jnp.int32)])
    pad_index = jnp.arange(DOCUMENT_TOKENS + LOOKBACK_SPAN, dtype=jnp.int32) - LOOKBACK_SPAN
    block_rows = T_SEQ
    span = LOOKBACK_SPAN + block_rows

    def one_block(block_id):
        start = (block_id * block_rows).astype(jnp.int32)
        query_block = lax.dynamic_slice_in_dim(query_matrix, start, block_rows, 0).astype(jnp.float32)
        query_places = lax.dynamic_slice_in_dim(positions.astype(jnp.int32), start, block_rows, 0)
        key_block = lax.dynamic_slice_in_dim(padded_keys, start, span, 0).astype(jnp.float32)
        value_block = lax.dynamic_slice_in_dim(padded_values, start, span, 0).astype(jnp.float32)
        key_places = lax.dynamic_slice_in_dim(pad_places, start, span, 0)
        key_index = lax.dynamic_slice_in_dim(pad_index, start, span, 0)
        distance = query_places[:, None] - key_places[None, :]
        allowed = (key_index[None, :] >= 0) & (distance >= 0) & (distance < LOOKBACK_SPAN)
        scores = jnp.einsum('qkgd,skd->kgqs', query_block, key_block) * score_scale
        weights = jnp.where(allowed[None, None], jnp.exp(scores), jnp.zeros_like(scores))
        total = lax.optimization_barrier(jnp.sum(weights, axis=-1))
        weights_b = lax.optimization_barrier(weights.astype(jnp.bfloat16)).astype(jnp.float32)
        summed = jnp.einsum('kgqs,skd->qkgd', weights_b, value_block)
        attended = summed / jnp.transpose(total, (2, 0, 1))[..., None]
        return attended.astype(jnp.bfloat16).reshape(block_rows, QUERY_HEADS * HEAD_SIZE)
    blocks = lax.map(one_block, jnp.arange(DOCUMENT_TOKENS // block_rows, dtype=jnp.int32))
    attended = blocks.reshape(DOCUMENT_TOKENS, QUERY_HEADS * HEAD_SIZE)
    group_cols = QUERY_HEADS * HEAD_SIZE // N_TP
    split_attended = attended.reshape(DOCUMENT_TOKENS, N_TP, group_cols)
    split_out = w_out.reshape(N_TP, group_cols, MODEL_WIDTH)

    def add_group(carry, index):
        left = lax.dynamic_index_in_dim(split_attended, index, 1, keepdims=False)
        right = lax.dynamic_index_in_dim(split_out, index, 0, keepdims=False)
        part = jnp.dot(left, right, preferred_element_type=jnp.float32).astype(jnp.bfloat16)
        part = lax.optimization_barrier(part)
        return (carry + part.astype(jnp.float32), None)
    attn_sum, _ = lax.scan(add_group, jnp.zeros((DOCUMENT_TOKENS, MODEL_WIDTH), jnp.float32), jnp.arange(N_TP, dtype=jnp.int32))
    return (stream + norm_scale(attn_sum, post_gain)).astype(jnp.bfloat16)
```

```python
import jax
import jax.numpy as jnp
from jax import lax
from jax.sharding import Mesh
from jax.sharding import PartitionSpec as P

LOOKBACK_SPAN = 1024


epsilon = 1e-06
score_scale = 168.0 ** (-0.5)
rotary_base = 10000.0


def from_behind(block, axis, distance):
    devices = range(lax.axis_size(axis))
    route = [(i - distance, i) for i in devices if i - distance in devices]
    return lax.ppermute(block, axis, route)


def norm_scale(value_matrix, gain):
    mean_square = jnp.mean(value_matrix * value_matrix, axis=-1, keepdims=True)
    return value_matrix * lax.rsqrt(mean_square + epsilon) * gain


def rotary(value_matrix, places):
    half_dim = value_matrix.shape[-1] // 2
    inverse = rotary_base ** (-jnp.arange(half_dim, dtype=jnp.float32) / half_dim)
    angles = places.astype(jnp.float32)[:, None] * inverse[None, :]
    cosine = jnp.cos(angles)[:, None, :]
    sine = jnp.sin(angles)[:, None, :]
    first = value_matrix[..., :half_dim]
    second = value_matrix[..., half_dim:]
    return jnp.concatenate(
        [first * cosine - second * sine, second * cosine + first * sine], axis=-1
    )


def local(
    residual,
    input_gain,
    w_query,
    key_weight,
    value_weight,
    query_gain,
    key_gain,
    w_out,
    post_gain,
    positions,
):
    tok_rows = residual.shape[0]
    seq_at = lax.axis_index("seq")
    tp_at = lax.axis_index("tp")
    head_dim = query_gain.shape[0]
    local_kv = key_weight.shape[1] // head_dim
    query_group = w_query.shape[1] // key_weight.shape[1]
    gathered = lax.all_gather(residual, "tp", axis=1, tiled=True)
    normalized_input = norm_scale(gathered.astype(jnp.float32), input_gain).astype(jnp.bfloat16)
    own_places = lax.dynamic_slice_in_dim(positions, seq_at * tok_rows, tok_rows, 0)
    reach = (LOOKBACK_SPAN - 2) // tok_rows + 1

    def attend(query_matrix, stacked, key_places, valid):
        key_matrix = stacked[0].reshape(-1, local_kv, head_dim)
        value_matrix = stacked[1].reshape(-1, local_kv, head_dim)
        scores = (
            jnp.einsum(
                "qkgd,skd->kgqs", query_matrix, key_matrix, preferred_element_type=jnp.float32
            )
            * score_scale
        )
        distance = own_places[:, None] - key_places[None, :]
        allowed = valid[None, :] & (distance >= 0) & (distance < LOOKBACK_SPAN)
        weights = jnp.where(allowed[None, None], jnp.exp(scores), jnp.zeros_like(scores))
        total = jnp.sum(weights, axis=-1)
        summed = jnp.einsum(
            "kgqs,skd->qkgd",
            weights.astype(jnp.bfloat16),
            value_matrix,
            preferred_element_type=jnp.float32,
        )
        return (total, summed)

    pieces = (
        lax.all_gather(w_query, "seq", axis=0, tiled=True),
        lax.all_gather(key_weight, "seq", axis=0, tiled=True),
        lax.all_gather(value_weight, "seq", axis=0, tiled=True),
    )
    queries_raw, unrotated_keys, projected_values = tuple(
        (jnp.dot(normalized_input, piece, preferred_element_type=jnp.float32) for piece in pieces)
    )
    key_matrix = rotary(
        norm_scale(unrotated_keys.reshape(tok_rows, local_kv, head_dim), key_gain), own_places
    )
    stacked = jnp.stack(
        [key_matrix.reshape(tok_rows, local_kv * head_dim), projected_values]
    ).astype(jnp.bfloat16)
    pieces = []
    for distance in range(reach, 0, -1):
        pieces.append(from_behind(stacked, "seq", distance))
    halo = jnp.concatenate(pieces, axis=1)
    query_matrix = rotary(
        norm_scale(queries_raw.reshape(tok_rows, local_kv * query_group, head_dim), query_gain),
        own_places,
    )
    query_matrix = query_matrix.astype(jnp.bfloat16).reshape(
        tok_rows, local_kv, query_group, head_dim
    )
    inner_total, inner_sum = attend(
        query_matrix, stacked, own_places, jnp.ones((tok_rows,), jnp.bool_)
    )
    span = halo.shape[1]
    padded_places = jnp.concatenate([jnp.zeros((span,), jnp.int32), positions])
    halo_places = lax.dynamic_slice_in_dim(padded_places, seq_at * tok_rows, span, 0)
    halo_valid = seq_at * tok_rows - span + jnp.arange(span, dtype=jnp.int32) >= 0
    outer_total, outer_sum = attend(query_matrix, halo, halo_places, halo_valid)
    total = jnp.transpose(inner_total + outer_total, (2, 0, 1))
    merged = (inner_sum + outer_sum) / total[..., None]
    attended = merged.astype(jnp.bfloat16).reshape(tok_rows, local_kv * query_group * head_dim)
    partial_out = jnp.dot(
        attended,
        lax.all_gather(w_out, "seq", axis=1, tiled=True),
        preferred_element_type=jnp.float32,
    )
    summed_cols = lax.psum_scatter(
        partial_out.astype(jnp.bfloat16), "tp", scatter_dimension=1, tiled=True
    ).astype(jnp.float32)
    full_width = post_gain.shape[0]
    squares = lax.psum(jnp.sum(summed_cols * summed_cols, axis=1), "tp")
    inverse_rms = lax.rsqrt(squares / full_width + epsilon)
    gain_part = lax.dynamic_slice_in_dim(
        post_gain, tp_at * summed_cols.shape[1], summed_cols.shape[1], 0
    )
    return (residual.astype(jnp.float32) + summed_cols * inverse_rms[:, None] * gain_part).astype(
        jnp.bfloat16
    )


def swap(block, axis):
    size = lax.axis_size(axis)
    return lax.ppermute(block, axis, [(i, i ^ 1) for i in range(size)])


def shift(block, axis, distance):
    size = lax.axis_size(axis)
    return lax.ppermute(block, axis, [(i, (i + distance) % size) for i in range(size)])


def pick(block, index, axis):
    return lax.dynamic_index_in_dim(block, index, axis, keepdims=False)


def in_order(at, own, other, axis=0):
    return jnp.stack(
        [jnp.where(at == 0, own, other), jnp.where(at == 0, other, own)], axis=axis
    )


def spread(weight):
    rows, _, _, cols = weight.shape
    z, x, c = lax.axis_index("z"), lax.axis_index("x"), lax.axis_index("c")
    planes = lax.axis_size("z")
    own = jnp.moveaxis(pick(weight, c, 2), 1, 0)
    other = swap(jnp.moveaxis(pick(weight, 1 - c, 2), 1, 0), "c")
    block = in_order(c, own, other, axis=1).reshape(2, 2 * rows, cols)
    pieces = [(z, pick(block, z % 2, 0))]
    for distance in range(1, planes):
        piece = pick(block, (z + distance) % 2, 0)
        pieces.append(((z - distance + planes) % planes, shift(piece, "z", distance)))
    whole = jnp.zeros((planes, 2, 2 * rows, cols), weight.dtype)
    for place, piece in pieces:
        across = swap(piece, "x")
        whole = lax.dynamic_update_slice(whole, piece[None, None], (place, x, 0, 0))
        whole = lax.dynamic_update_slice(whole, across[None, None], (place, 1 - x, 0, 0))
    return whole.reshape(planes * 4 * rows, cols)


def rearranged(
    residual,
    input_gain,
    w_query,
    key_weight,
    value_weight,
    query_gain,
    key_gain,
    w_out,
    post_gain,
    positions,
):
    tok, half_width = residual.shape
    head_dim = query_gain.shape[0]
    z, x, c = lax.axis_index("z"), lax.axis_index("x"), lax.axis_index("c")
    y = lax.axis_index("y")
    pair, zz = z // 2, z % 2
    rows = w_query.shape[0]
    kv_cols = key_weight.shape[1] // 4
    q_cols = w_query.shape[1] // 4
    kv_heads = kv_cols // head_dim
    group = q_cols // kv_cols
    run = 2 * tok
    full_width = 2 * half_width

    stream = residual.astype(jnp.float32)
    squares = jnp.sum(stream * stream, axis=1, keepdims=True)
    squares = squares + swap(squares, "y")
    gain_in = lax.dynamic_slice_in_dim(input_gain, y * half_width, half_width, 0)
    normed = (stream * lax.rsqrt(squares / full_width + epsilon) * gain_in).astype(jnp.bfloat16)
    normed = in_order(zz, normed, swap(normed, "z"))
    other = swap(normed, "y")
    normed = jnp.concatenate(
        [jnp.where(y == 0, normed, other), jnp.where(y == 0, other, normed)], axis=-1
    )
    normed = in_order(c, normed, swap(normed, "c"), axis=1).reshape(2 * run, full_width)

    kv_weight = jnp.concatenate(
        [
            key_weight.reshape(rows, 2, 2, kv_cols),
            value_weight.reshape(rows, 2, 2, kv_cols),
        ],
        axis=-1,
    )
    kv_all = spread(kv_weight)
    q_all = spread(w_query.reshape(rows, 2, 2, q_cols))
    o_all = spread(w_out.T.reshape(rows, 2, 2, q_cols))

    def places_of(i):
        return lax.dynamic_slice_in_dim(positions, (4 * pair + 2 * i + x) * run, run, 0)

    places = jnp.concatenate([places_of(0), places_of(1)])
    kv_raw = jnp.dot(normed, kv_all, preferred_element_type=jnp.float32)
    keys = rotary(
        norm_scale(kv_raw[:, :kv_cols].reshape(2 * run, kv_heads, head_dim), key_gain), places
    ).reshape(2 * run, kv_cols)
    kv = jnp.concatenate([keys, kv_raw[:, kv_cols:]], axis=1).astype(jnp.bfloat16)
    kv = kv.reshape(2, run, 2 * kv_cols)
    before = from_behind(kv[1], "z", 2)
    own = jnp.concatenate([before[None], kv])
    across = jnp.concatenate([swap(before, "x")[None], swap(kv, "x")])
    kv_runs = in_order(x, own, across, axis=1).reshape(6 * run, 2 * kv_cols)
    key_places = lax.dynamic_slice_in_dim(
        jnp.concatenate([jnp.zeros((2 * run,), jnp.int32), positions]), 4 * pair * run, 6 * run, 0
    )
    key_index = (4 * pair - 2) * run + jnp.arange(6 * run, dtype=jnp.int32)
    key_places = jnp.where(key_index >= 0, key_places, jnp.int32(1 << 30))

    q_raw = jnp.dot(normed, q_all, preferred_element_type=jnp.float32)
    queries = rotary(
        norm_scale(q_raw.reshape(2 * run, kv_heads * group, head_dim), query_gain), places
    ).astype(jnp.bfloat16)
    queries = queries.reshape(2, run, kv_heads, group, head_dim)

    def attend(i):
        start = (2 * i + x) * run
        window = lax.dynamic_slice_in_dim(kv_runs, start, 3 * run, 0)
        window_places = lax.dynamic_slice_in_dim(key_places, start, 3 * run, 0)
        window_keys = window[:, :kv_cols].reshape(3 * run, kv_heads, head_dim)
        window_values = window[:, kv_cols:].reshape(3 * run, kv_heads, head_dim)
        scores = (
            jnp.einsum(
                "qkgd,skd->kgqs", queries[i], window_keys, preferred_element_type=jnp.float32
            )
            * score_scale
        )
        distance = places_of(i)[:, None] - window_places[None, :]
        allowed = (distance >= 0) & (distance < LOOKBACK_SPAN)
        weights = jnp.where(allowed[None, None], jnp.exp(scores), jnp.zeros_like(scores))
        total = jnp.sum(weights, axis=-1)
        summed = jnp.einsum(
            "kgqs,skd->qkgd",
            weights.astype(jnp.bfloat16),
            window_values,
            preferred_element_type=jnp.float32,
        )
        merged = summed / jnp.transpose(total, (2, 0, 1))[..., None]
        return merged.astype(jnp.bfloat16).reshape(run, q_cols)

    attended = jnp.concatenate([attend(0), attend(1)])

    cut = (half_width // 2 + 127) // 128 * 128
    o_halves = o_all.reshape(2, half_width, q_cols)
    sums = []
    for low, high, z_first in ((0, cut, True), (cut, half_width, False)):
        width = high - low
        part = lax.dot_general(
            attended,
            o_halves[:, low:high].reshape(2 * width, q_cols),
            (((1,), (1,)), ((), ())),
            preferred_element_type=jnp.float32,
        )
        part = part.reshape(2, 2, tok, 2 * width)
        part = pick(part, c, 1) + swap(pick(part, 1 - c, 1).astype(jnp.bfloat16), "c").astype(
            jnp.float32
        )
        part = part.reshape(2, tok, 2, width)
        for axis in ("z", "y") if z_first else ("y", "z"):
            at, dim = (zz, 0) if axis == "z" else (y, part.ndim - 2)
            part = pick(part, at, dim) + swap(
                pick(part, 1 - at, dim).astype(jnp.bfloat16), axis
            ).astype(jnp.float32)
        sums.append(part)
    attn_sum = jnp.concatenate(sums, axis=1)
    squares = jnp.sum(attn_sum * attn_sum, axis=1, keepdims=True)
    squares = squares + swap(squares, "y")
    gain_out = lax.dynamic_slice_in_dim(post_gain, y * half_width, half_width, 0)
    return (stream + attn_sum * lax.rsqrt(squares / full_width + epsilon) * gain_out).astype(
        jnp.bfloat16
    )


def solution(mesh):
    seq, tp = mesh.shape["seq"], mesh.shape["tp"]
    if tp == 2 and seq % 8 == 0:
        mesh = Mesh(mesh.devices.reshape(seq // 4, 2, 2, tp), ("z", "x", "c", "y"))
        seq_axes, tp_axes, body = ("z", "x", "c"), "y", rearranged
    else:
        seq_axes, tp_axes, body = "seq", "tp", local
    in_specs = (
        P(seq_axes, tp_axes),
        P(),
        P(seq_axes, tp_axes),
        P(seq_axes, tp_axes),
        P(seq_axes, tp_axes),
        P(),
        P(),
        P(tp_axes, seq_axes),
        P(),
        P(),
    )
    out_specs = P(seq_axes, tp_axes)
    return jax.shard_map(body, mesh=mesh, in_specs=in_specs, out_specs=out_specs, check_vma=False)
```

```python
import functools

import jax
import jax.numpy as jnp
from jax import lax
from jax.experimental import pallas as pl
from jax.experimental.pallas import tpu as pltpu
from jax.sharding import Mesh
from jax.sharding import PartitionSpec as P

LOOKBACK_SPAN = 1024


epsilon = 1e-06
score_scale = 168.0 ** (-0.5)
rotary_base = 10000.0


def from_behind(block, axis, distance):
    devices = range(lax.axis_size(axis))
    route = [(i - distance, i) for i in devices if i - distance in devices]
    return lax.ppermute(block, axis, route)


def norm_scale(value_matrix, gain):
    mean_square = jnp.mean(value_matrix * value_matrix, axis=-1, keepdims=True)
    return value_matrix * lax.rsqrt(mean_square + epsilon) * gain


def rotary(value_matrix, places):
    half_dim = value_matrix.shape[-1] // 2
    inverse = rotary_base ** (-jnp.arange(half_dim, dtype=jnp.float32) / half_dim)
    angles = places.astype(jnp.float32)[:, None] * inverse[None, :]
    cosine = jnp.cos(angles)[:, None, :]
    sine = jnp.sin(angles)[:, None, :]
    first = value_matrix[..., :half_dim]
    second = value_matrix[..., half_dim:]
    return jnp.concatenate(
        [first * cosine - second * sine, second * cosine + first * sine], axis=-1
    )


def local(
    residual,
    input_gain,
    w_query,
    key_weight,
    value_weight,
    query_gain,
    key_gain,
    w_out,
    post_gain,
    positions,
):
    tok_rows = residual.shape[0]
    seq_at = lax.axis_index("seq")
    tp_at = lax.axis_index("tp")
    head_dim = query_gain.shape[0]
    local_kv = key_weight.shape[1] // head_dim
    query_group = w_query.shape[1] // key_weight.shape[1]
    gathered = lax.all_gather(residual, "tp", axis=1, tiled=True)
    normalized_input = norm_scale(gathered.astype(jnp.float32), input_gain).astype(jnp.bfloat16)
    own_places = lax.dynamic_slice_in_dim(positions, seq_at * tok_rows, tok_rows, 0)
    reach = (LOOKBACK_SPAN - 2) // tok_rows + 1

    def attend(query_matrix, stacked, key_places, valid):
        key_matrix = stacked[0].reshape(-1, local_kv, head_dim)
        value_matrix = stacked[1].reshape(-1, local_kv, head_dim)
        scores = (
            jnp.einsum(
                "qkgd,skd->kgqs", query_matrix, key_matrix, preferred_element_type=jnp.float32
            )
            * score_scale
        )
        distance = own_places[:, None] - key_places[None, :]
        allowed = valid[None, :] & (distance >= 0) & (distance < LOOKBACK_SPAN)
        weights = jnp.where(allowed[None, None], jnp.exp(scores), jnp.zeros_like(scores))
        total = jnp.sum(weights, axis=-1)
        summed = jnp.einsum(
            "kgqs,skd->qkgd",
            weights.astype(jnp.bfloat16),
            value_matrix,
            preferred_element_type=jnp.float32,
        )
        return (total, summed)

    pieces = (
        lax.all_gather(w_query, "seq", axis=0, tiled=True),
        lax.all_gather(key_weight, "seq", axis=0, tiled=True),
        lax.all_gather(value_weight, "seq", axis=0, tiled=True),
    )
    queries_raw, unrotated_keys, projected_values = tuple(
        (jnp.dot(normalized_input, piece, preferred_element_type=jnp.float32) for piece in pieces)
    )
    key_matrix = rotary(
        norm_scale(unrotated_keys.reshape(tok_rows, local_kv, head_dim), key_gain), own_places
    )
    stacked = jnp.stack(
        [key_matrix.reshape(tok_rows, local_kv * head_dim), projected_values]
    ).astype(jnp.bfloat16)
    pieces = []
    for distance in range(reach, 0, -1):
        pieces.append(from_behind(stacked, "seq", distance))
    halo = jnp.concatenate(pieces, axis=1)
    query_matrix = rotary(
        norm_scale(queries_raw.reshape(tok_rows, local_kv * query_group, head_dim), query_gain),
        own_places,
    )
    query_matrix = query_matrix.astype(jnp.bfloat16).reshape(
        tok_rows, local_kv, query_group, head_dim
    )
    inner_total, inner_sum = attend(
        query_matrix, stacked, own_places, jnp.ones((tok_rows,), jnp.bool_)
    )
    span = halo.shape[1]
    padded_places = jnp.concatenate([jnp.zeros((span,), jnp.int32), positions])
    halo_places = lax.dynamic_slice_in_dim(padded_places, seq_at * tok_rows, span, 0)
    halo_valid = seq_at * tok_rows - span + jnp.arange(span, dtype=jnp.int32) >= 0
    outer_total, outer_sum = attend(query_matrix, halo, halo_places, halo_valid)
    total = jnp.transpose(inner_total + outer_total, (2, 0, 1))
    merged = (inner_sum + outer_sum) / total[..., None]
    attended = merged.astype(jnp.bfloat16).reshape(tok_rows, local_kv * query_group * head_dim)
    partial_out = jnp.dot(
        attended,
        lax.all_gather(w_out, "seq", axis=1, tiled=True),
        preferred_element_type=jnp.float32,
    )
    summed_cols = lax.psum_scatter(
        partial_out.astype(jnp.bfloat16), "tp", scatter_dimension=1, tiled=True
    ).astype(jnp.float32)
    full_width = post_gain.shape[0]
    squares = lax.psum(jnp.sum(summed_cols * summed_cols, axis=1), "tp")
    inverse_rms = lax.rsqrt(squares / full_width + epsilon)
    gain_part = lax.dynamic_slice_in_dim(
        post_gain, tp_at * summed_cols.shape[1], summed_cols.shape[1], 0
    )
    return (residual.astype(jnp.float32) + summed_cols * inverse_rms[:, None] * gain_part).astype(
        jnp.bfloat16
    )


def swap(block, axis):
    size = lax.axis_size(axis)
    return lax.ppermute(block, axis, [(i, i ^ 1) for i in range(size)])


def shift(block, axis, distance):
    size = lax.axis_size(axis)
    return lax.ppermute(block, axis, [(i, (i + distance) % size) for i in range(size)])


def pick(block, index, axis):
    return lax.dynamic_index_in_dim(block, index, axis, keepdims=False)


def in_order(at, own, other, axis=0):
    return jnp.stack(
        [jnp.where(at == 0, own, other), jnp.where(at == 0, other, own)], axis=axis
    )


def gather_kernel(
    planes,
    x_ref,
    wk_ref,
    wv_ref,
    wq_ref,
    wo_ref,
    kv_ref,
    q_ref,
    o_ref,
    x_all,
    kv_all,
    q_all,
    x_send,
    x_recv,
    w_send,
    w_recv,
    f_send,
    f_recv,
    local_sem,
):
    z, x, c = lax.axis_index("z"), lax.axis_index("x"), lax.axis_index("c")
    y = lax.axis_index("y")
    zz = lax.rem(z, 2)
    rels = [(dz, dc) for dz in range(planes) for dc in range(2)]

    def at(dz, dc):
        return lax.rem(z + dz + planes, planes), lax.rem(c + dc + 2, 2)

    def device(dz, dc):
        there_z, there_c = at(dz, dc)
        return (there_z, x, there_c, y)

    x_mate = (z, 1 - x, c, y)
    y_mate = (z, x, c, 1 - y)
    c_mate = (z, x, 1 - c, y)
    z_mate = (z + 1 - 2 * zz, x, c, y)

    barrier = pltpu.get_barrier_semaphore()
    peers = [device(*rel) for rel in rels[1:]] + [x_mate, y_mate]
    for peer in peers:
        pl.semaphore_signal(barrier, inc=1, device_id=peer, device_id_type=pl.DeviceIdType.MESH)
    pl.semaphore_wait(barrier, len(peers))

    def remote(src, dst, send, recv, to):
        return pltpu.make_async_remote_copy(
            src_ref=src,
            dst_ref=dst,
            send_sem=send,
            recv_sem=recv,
            device_id=to,
            device_id_type=pl.DeviceIdType.MESH,
        )

    kv_cols = wk_ref.shape[1] // 4
    q_cols = wq_ref.shape[1] // 4
    weights = (
        (wk_ref, kv_all, 0, kv_cols),
        (wv_ref, kv_all, kv_cols, kv_cols),
        (wq_ref, q_all, 0, q_cols),
        (wo_ref, o_ref, 0, q_cols),
    )

    def slot(t, dz, dc, side):
        there_z, there_c = at(-dz, -dc)
        _, buf, low, cols = weights[t]
        return buf.at[(there_z * 2 + side) * 2 + there_c, :, pl.ds(low, cols)]

    def columns(t, dz, dc):
        there_z, there_c = at(dz, dc)
        ref, _, _, cols = weights[t]
        first = pl.multiple_of((lax.rem(there_z, 2) * 2 + there_c) * cols, cols)
        return ref.at[:, pl.ds(first, cols)]

    def send(t, i):
        return remote(
            columns(t, *rels[i]), slot(t, 0, 0, x), w_send.at[t, i], w_recv.at[t, i], device(*rels[i])
        )

    def arrived(t, i):
        here = slot(t, *rels[i], x)
        return remote(here, here, w_send.at[t, i], w_recv.at[t, i], device(*rels[i]))

    def forward(t, i):
        here = slot(t, *rels[i], x)
        source = columns(t, 0, 0) if i == 0 else here
        return remote(source, here, f_send.at[t, i], f_recv.at[t, i], x_mate)

    def forwarded(t, i):
        here = slot(t, *rels[i], 1 - x)
        return remote(here, here, f_send.at[t, i], f_recv.at[t, i], x_mate)

    chunks = x_ref.shape[0]

    def x_slot(row, core, half):
        return x_all.at[pl.ds(half * chunks, chunks), row * 2 + core]

    def x_copy(i, source, row, half, to):
        return remote(source, x_slot(row, c, half), x_send.at[i], x_recv.at[i], to)

    def x_arrived(i, row, core, half):
        here = x_slot(row, core, half)
        return remote(here, here, x_send.at[i], x_recv.at[i], z_mate)

    def own(t):
        return pltpu.make_async_copy(columns(t, 0, 0), slot(t, 0, 0, x), local_sem.at[t])

    own_x = pltpu.make_async_copy(x_ref, x_slot(zz, c, y), local_sem.at[4])
    x_copies = [
        x_copy(0, x_ref, zz, y, z_mate),
        x_copy(1, x_ref, zz, y, y_mate),
        x_copy(2, x_ref, zz, y, c_mate),
    ]
    for copy in x_copies:
        copy.start()
    own_x.start()
    for t in (0, 1, 2, 3):
        own(t).start()

    def send_all(t):
        for i in range(1, len(rels)):
            send(t, i).start()
        forward(t, 0).start()

    def forward_all(t):
        for i in range(1, len(rels)):
            arrived(t, i).wait_recv()
            forward(t, i).start()

    send_all(0)
    send_all(1)
    x_arrived(0, 1 - zz, c, y).wait_recv()
    x_copies.append(x_copy(3, x_slot(1 - zz, c, y), 1 - zz, y, y_mate))
    x_copies.append(x_copy(4, x_slot(1 - zz, c, y), 1 - zz, y, c_mate))
    for copy in x_copies[3:]:
        copy.start()
    send_all(2)
    x_arrived(1, zz, c, 1 - y).wait_recv()
    x_copies.append(x_copy(5, x_slot(zz, c, 1 - y), zz, 1 - y, c_mate))
    x_copies[5].start()
    forward_all(0)
    forward_all(1)
    x_arrived(3, 1 - zz, c, 1 - y).wait_recv()
    x_copies.append(x_copy(6, x_slot(1 - zz, c, 1 - y), 1 - zz, 1 - y, c_mate))
    x_copies[6].start()
    send_all(3)
    forward_all(2)

    x_arrived(2, zz, 1 - c, y).wait_recv()
    x_arrived(4, 1 - zz, 1 - c, y).wait_recv()
    x_arrived(5, zz, 1 - c, 1 - y).wait_recv()
    x_arrived(6, 1 - zz, 1 - c, 1 - y).wait_recv()
    own_x.wait()

    def multiply(weight, out_ref):
        blocks, tok = x_all.shape[1], x_all.shape[2]
        out_ref[...] = jnp.zeros_like(out_ref)

        def one(step, carry):
            j, k = step // blocks, step % blocks
            rows = pl.ds(pl.multiple_of(k * tok, tok), tok)
            out_ref[rows, :] += jnp.dot(
                x_all[j, k], weight[j], preferred_element_type=jnp.float32
            )
            return carry

        lax.fori_loop(0, x_all.shape[0] * blocks, one, 0)

    for t in (0, 1):
        own(t).wait()
        for i in range(len(rels)):
            forwarded(t, i).wait_recv()
    multiply(kv_all, kv_ref)
    forward_all(3)
    own(2).wait()
    for i in range(len(rels)):
        forwarded(2, i).wait_recv()
    multiply(q_all, q_ref)
    own(3).wait()
    for i in range(len(rels)):
        forwarded(3, i).wait_recv()
    for copy in x_copies:
        copy.wait_send()
    for t in range(4):
        for i in range(len(rels)):
            if i > 0:
                send(t, i).wait_send()
            forward(t, i).wait_send()


def gathered_products(normed, key_weight, value_weight, w_query, w_out):
    tok, half_width = normed.shape
    rows = key_weight.shape[0]
    planes = lax.axis_size("z")
    kv_cols, q_cols = key_weight.shape[1] // 2, w_query.shape[1] // 4
    places = planes * 4
    chunks = half_width // rows
    split = jnp.transpose(normed.reshape(tok, chunks, rows), (1, 0, 2))
    any_space = pl.BlockSpec(memory_space=pl.ANY)
    vmem_space = pl.BlockSpec(memory_space=pltpu.VMEM)
    dma = pltpu.SemaphoreType.DMA
    kv_raw, q_raw, o_all = pl.pallas_call(
        functools.partial(gather_kernel, planes),
        out_shape=(
            jax.ShapeDtypeStruct((4 * tok, kv_cols), jnp.float32),
            jax.ShapeDtypeStruct((4 * tok, q_cols), jnp.float32),
            jax.ShapeDtypeStruct((places, rows, q_cols), jnp.bfloat16),
        ),
        in_specs=[any_space] * 5,
        out_specs=(vmem_space, vmem_space, any_space),
        scratch_shapes=[
            pltpu.VMEM((places, 4, tok, rows), jnp.bfloat16),
            pltpu.VMEM((places, rows, kv_cols), jnp.bfloat16),
            pltpu.VMEM((places, rows, q_cols), jnp.bfloat16),
            dma((7,)),
            dma((7,)),
            dma((4, places // 2)),
            dma((4, places // 2)),
            dma((4, places // 2)),
            dma((4, places // 2)),
            dma((5,)),
        ],
        compiler_params=pltpu.CompilerParams(
            collective_id=0, has_side_effects=True, vmem_limit_bytes=44 << 20
        ),
    )(split, key_weight, value_weight, w_query, w_out)
    return kv_raw, q_raw, o_all.reshape(places * rows, q_cols)


def rearranged(
    residual,
    input_gain,
    w_query,
    key_weight,
    value_weight,
    query_gain,
    key_gain,
    w_out,
    post_gain,
    positions,
):
    tok, half_width = residual.shape
    head_dim = query_gain.shape[0]
    z, x, c = lax.axis_index("z"), lax.axis_index("x"), lax.axis_index("c")
    y = lax.axis_index("y")
    pair, zz = z // 2, z % 2
    kv_cols = key_weight.shape[1] // 4
    q_cols = w_query.shape[1] // 4
    kv_heads = kv_cols // head_dim
    group = q_cols // kv_cols
    run = 2 * tok
    full_width = 2 * half_width

    stream = residual.astype(jnp.float32)
    squares = jnp.sum(stream * stream, axis=1, keepdims=True)
    squares = squares + swap(squares, "y")
    gain_in = lax.dynamic_slice_in_dim(input_gain, y * half_width, half_width, 0)
    normed = (stream * lax.rsqrt(squares / full_width + epsilon) * gain_in).astype(jnp.bfloat16)
    kv_raw, q_raw, o_all = gathered_products(
        normed, key_weight, value_weight, w_query, w_out.T
    )

    def places_of(i):
        return lax.dynamic_slice_in_dim(positions, (4 * pair + 2 * i + x) * run, run, 0)

    places = jnp.concatenate([places_of(0), places_of(1)])
    keys = rotary(
        norm_scale(kv_raw[:, :kv_cols].reshape(2 * run, kv_heads, head_dim), key_gain), places
    ).reshape(2 * run, kv_cols)
    kv = jnp.concatenate([keys, kv_raw[:, kv_cols:]], axis=1).astype(jnp.bfloat16)
    kv = kv.reshape(2, run, 2 * kv_cols)
    before = from_behind(kv[1], "z", 2)
    own = jnp.concatenate([before[None], kv])
    across = jnp.concatenate([swap(before, "x")[None], swap(kv, "x")])
    kv_runs = in_order(x, own, across, axis=1).reshape(6 * run, 2 * kv_cols)
    key_places = lax.dynamic_slice_in_dim(
        jnp.concatenate([jnp.zeros((2 * run,), jnp.int32), positions]), 4 * pair * run, 6 * run, 0
    )
    key_index = (4 * pair - 2) * run + jnp.arange(6 * run, dtype=jnp.int32)
    key_places = jnp.where(key_index >= 0, key_places, jnp.int32(1 << 30))

    queries = rotary(
        norm_scale(q_raw.reshape(2 * run, kv_heads * group, head_dim), query_gain), places
    ).astype(jnp.bfloat16)
    queries = queries.reshape(2, run, kv_heads, group, head_dim)

    def attend(i):
        start = (2 * i + x) * run
        window = lax.dynamic_slice_in_dim(kv_runs, start, 3 * run, 0)
        window_places = lax.dynamic_slice_in_dim(key_places, start, 3 * run, 0)
        window_keys = window[:, :kv_cols].reshape(3 * run, kv_heads, head_dim)
        window_values = window[:, kv_cols:].reshape(3 * run, kv_heads, head_dim)
        scores = (
            jnp.einsum(
                "qkgd,skd->kgqs", queries[i], window_keys, preferred_element_type=jnp.float32
            )
            * score_scale
        )
        distance = places_of(i)[:, None] - window_places[None, :]
        allowed = (distance >= 0) & (distance < LOOKBACK_SPAN)
        weights = jnp.where(allowed[None, None], jnp.exp(scores), jnp.zeros_like(scores))
        total = jnp.sum(weights, axis=-1)
        summed = jnp.einsum(
            "kgqs,skd->qkgd",
            weights.astype(jnp.bfloat16),
            window_values,
            preferred_element_type=jnp.float32,
        )
        merged = summed / jnp.transpose(total, (2, 0, 1))[..., None]
        return merged.astype(jnp.bfloat16).reshape(run, q_cols)

    attended = jnp.concatenate([attend(0), attend(1)])

    cut = (half_width // 2 + 127) // 128 * 128
    o_halves = o_all.reshape(2, half_width, q_cols)
    sums = []
    for low, high, z_first in ((0, cut, True), (cut, half_width, False)):
        width = high - low
        part = lax.dot_general(
            attended,
            o_halves[:, low:high].reshape(2 * width, q_cols),
            (((1,), (1,)), ((), ())),
            preferred_element_type=jnp.float32,
        )
        part = part.reshape(2, 2, tok, 2 * width)
        part = pick(part, c, 1) + swap(pick(part, 1 - c, 1).astype(jnp.bfloat16), "c").astype(
            jnp.float32
        )
        part = part.reshape(2, tok, 2, width)
        for axis in ("z", "y") if z_first else ("y", "z"):
            at, dim = (zz, 0) if axis == "z" else (y, part.ndim - 2)
            part = pick(part, at, dim) + swap(
                pick(part, 1 - at, dim).astype(jnp.bfloat16), axis
            ).astype(jnp.float32)
        sums.append(part)
    attn_sum = jnp.concatenate(sums, axis=1)
    squares = jnp.sum(attn_sum * attn_sum, axis=1, keepdims=True)
    squares = squares + swap(squares, "y")
    gain_out = lax.dynamic_slice_in_dim(post_gain, y * half_width, half_width, 0)
    return (stream + attn_sum * lax.rsqrt(squares / full_width + epsilon) * gain_out).astype(
        jnp.bfloat16
    )


def solution(mesh):
    seq, tp = mesh.shape["seq"], mesh.shape["tp"]
    if tp == 2 and seq % 8 == 0:
        mesh = Mesh(mesh.devices.reshape(seq // 4, 2, 2, tp), ("z", "x", "c", "y"))
        seq_axes, tp_axes, body = ("z", "x", "c"), "y", rearranged
    else:
        seq_axes, tp_axes, body = "seq", "tp", local
    in_specs = (
        P(seq_axes, tp_axes),
        P(),
        P(seq_axes, tp_axes),
        P(seq_axes, tp_axes),
        P(seq_axes, tp_axes),
        P(),
        P(),
        P(tp_axes, seq_axes),
        P(),
        P(),
    )
    out_specs = P(seq_axes, tp_axes)
    return jax.shard_map(body, mesh=mesh, in_specs=in_specs, out_specs=out_specs, check_vma=False)
```

```python
import functools

import jax
import jax.numpy as jnp
from jax import lax
from jax.experimental import pallas as pl
from jax.experimental.pallas import tpu as pltpu
from jax.sharding import Mesh
from jax.sharding import PartitionSpec as P

LOOKBACK_SPAN = 1024


epsilon = 1e-06
score_scale = 168.0 ** (-0.5)
rotary_base = 10000.0


def from_behind(block, axis, distance):
    devices = range(lax.axis_size(axis))
    route = [(i - distance, i) for i in devices if i - distance in devices]
    return lax.ppermute(block, axis, route)


def norm_scale(value_matrix, gain):
    mean_square = jnp.mean(value_matrix * value_matrix, axis=-1, keepdims=True)
    return value_matrix * lax.rsqrt(mean_square + epsilon) * gain


def rotary(value_matrix, places):
    half_dim = value_matrix.shape[-1] // 2
    inverse = rotary_base ** (-jnp.arange(half_dim, dtype=jnp.float32) / half_dim)
    angles = places.astype(jnp.float32)[:, None] * inverse[None, :]
    cosine = jnp.cos(angles)[:, None, :]
    sine = jnp.sin(angles)[:, None, :]
    first = value_matrix[..., :half_dim]
    second = value_matrix[..., half_dim:]
    return jnp.concatenate(
        [first * cosine - second * sine, second * cosine + first * sine], axis=-1
    )


def local(
    residual,
    input_gain,
    w_query,
    key_weight,
    value_weight,
    query_gain,
    key_gain,
    w_out,
    post_gain,
    positions,
):
    tok_rows = residual.shape[0]
    seq_at = lax.axis_index("seq")
    tp_at = lax.axis_index("tp")
    head_dim = query_gain.shape[0]
    local_kv = key_weight.shape[1] // head_dim
    query_group = w_query.shape[1] // key_weight.shape[1]
    gathered = lax.all_gather(residual, "tp", axis=1, tiled=True)
    normalized_input = norm_scale(gathered.astype(jnp.float32), input_gain).astype(jnp.bfloat16)
    own_places = lax.dynamic_slice_in_dim(positions, seq_at * tok_rows, tok_rows, 0)
    reach = (LOOKBACK_SPAN - 2) // tok_rows + 1

    def attend(query_matrix, stacked, key_places, valid):
        key_matrix = stacked[0].reshape(-1, local_kv, head_dim)
        value_matrix = stacked[1].reshape(-1, local_kv, head_dim)
        scores = (
            jnp.einsum(
                "qkgd,skd->kgqs", query_matrix, key_matrix, preferred_element_type=jnp.float32
            )
            * score_scale
        )
        distance = own_places[:, None] - key_places[None, :]
        allowed = valid[None, :] & (distance >= 0) & (distance < LOOKBACK_SPAN)
        weights = jnp.where(allowed[None, None], jnp.exp(scores), jnp.zeros_like(scores))
        total = jnp.sum(weights, axis=-1)
        summed = jnp.einsum(
            "kgqs,skd->qkgd",
            weights.astype(jnp.bfloat16),
            value_matrix,
            preferred_element_type=jnp.float32,
        )
        return (total, summed)

    pieces = (
        lax.all_gather(w_query, "seq", axis=0, tiled=True),
        lax.all_gather(key_weight, "seq", axis=0, tiled=True),
        lax.all_gather(value_weight, "seq", axis=0, tiled=True),
    )
    queries_raw, unrotated_keys, projected_values = tuple(
        (jnp.dot(normalized_input, piece, preferred_element_type=jnp.float32) for piece in pieces)
    )
    key_matrix = rotary(
        norm_scale(unrotated_keys.reshape(tok_rows, local_kv, head_dim), key_gain), own_places
    )
    stacked = jnp.stack(
        [key_matrix.reshape(tok_rows, local_kv * head_dim), projected_values]
    ).astype(jnp.bfloat16)
    pieces = []
    for distance in range(reach, 0, -1):
        pieces.append(from_behind(stacked, "seq", distance))
    halo = jnp.concatenate(pieces, axis=1)
    query_matrix = rotary(
        norm_scale(queries_raw.reshape(tok_rows, local_kv * query_group, head_dim), query_gain),
        own_places,
    )
    query_matrix = query_matrix.astype(jnp.bfloat16).reshape(
        tok_rows, local_kv, query_group, head_dim
    )
    inner_total, inner_sum = attend(
        query_matrix, stacked, own_places, jnp.ones((tok_rows,), jnp.bool_)
    )
    span = halo.shape[1]
    padded_places = jnp.concatenate([jnp.zeros((span,), jnp.int32), positions])
    halo_places = lax.dynamic_slice_in_dim(padded_places, seq_at * tok_rows, span, 0)
    halo_valid = seq_at * tok_rows - span + jnp.arange(span, dtype=jnp.int32) >= 0
    outer_total, outer_sum = attend(query_matrix, halo, halo_places, halo_valid)
    total = jnp.transpose(inner_total + outer_total, (2, 0, 1))
    merged = (inner_sum + outer_sum) / total[..., None]
    attended = merged.astype(jnp.bfloat16).reshape(tok_rows, local_kv * query_group * head_dim)
    partial_out = jnp.dot(
        attended,
        lax.all_gather(w_out, "seq", axis=1, tiled=True),
        preferred_element_type=jnp.float32,
    )
    summed_cols = lax.psum_scatter(
        partial_out.astype(jnp.bfloat16), "tp", scatter_dimension=1, tiled=True
    ).astype(jnp.float32)
    full_width = post_gain.shape[0]
    squares = lax.psum(jnp.sum(summed_cols * summed_cols, axis=1), "tp")
    inverse_rms = lax.rsqrt(squares / full_width + epsilon)
    gain_part = lax.dynamic_slice_in_dim(
        post_gain, tp_at * summed_cols.shape[1], summed_cols.shape[1], 0
    )
    return (residual.astype(jnp.float32) + summed_cols * inverse_rms[:, None] * gain_part).astype(
        jnp.bfloat16
    )


def swap(block, axis):
    size = lax.axis_size(axis)
    return lax.ppermute(block, axis, [(i, i ^ 1) for i in range(size)])


def shift(block, axis, distance):
    size = lax.axis_size(axis)
    return lax.ppermute(block, axis, [(i, (i + distance) % size) for i in range(size)])


def pick(block, index, axis):
    return lax.dynamic_index_in_dim(block, index, axis, keepdims=False)


def in_order(at, own, other, axis=0):
    return jnp.stack(
        [jnp.where(at == 0, own, other), jnp.where(at == 0, other, own)], axis=axis
    )


def gather_kernel(
    planes,
    x_ref,
    wk_ref,
    wv_ref,
    wq_ref,
    wo_ref,
    kv_ref,
    q_ref,
    o_ref,
    x_all,
    kv_all,
    q_all,
    x_send,
    x_recv,
    w_send,
    w_recv,
    f_send,
    f_recv,
    local_sem,
):
    z, x, c = lax.axis_index("z"), lax.axis_index("x"), lax.axis_index("c")
    y = lax.axis_index("y")
    zz = lax.rem(z, 2)
    rels = [(dz, dc) for dz in range(planes) for dc in range(2)]

    def at(dz, dc):
        return lax.rem(z + dz + planes, planes), lax.rem(c + dc + 2, 2)

    def device(dz, dc):
        there_z, there_c = at(dz, dc)
        return (there_z, x, there_c, y)

    x_mate = (z, 1 - x, c, y)
    y_mate = (z, x, c, 1 - y)
    c_mate = (z, x, 1 - c, y)
    z_mate = (z + 1 - 2 * zz, x, c, y)

    barrier = pltpu.get_barrier_semaphore()
    peers = [device(*rel) for rel in rels[1:]] + [x_mate, y_mate]
    for peer in peers:
        pl.semaphore_signal(barrier, inc=1, device_id=peer, device_id_type=pl.DeviceIdType.MESH)
    pl.semaphore_wait(barrier, len(peers))

    def remote(src, dst, send, recv, to):
        return pltpu.make_async_remote_copy(
            src_ref=src,
            dst_ref=dst,
            send_sem=send,
            recv_sem=recv,
            device_id=to,
            device_id_type=pl.DeviceIdType.MESH,
        )

    kv_cols = wk_ref.shape[1] // 4
    q_cols = wq_ref.shape[1] // 4
    weights = (
        (wk_ref, kv_all, 0, kv_cols),
        (wv_ref, kv_all, kv_cols, kv_cols),
        (wq_ref, q_all, 0, q_cols),
        (wo_ref, o_ref, 0, q_cols),
    )

    def slot(t, dz, dc, side):
        there_z, there_c = at(-dz, -dc)
        _, buf, low, cols = weights[t]
        if t == 3:
            there_z = lax.rem(there_z + y * (planes // 2), planes)
        return buf.at[(there_z * 2 + side) * 2 + there_c, :, pl.ds(low, cols)]

    def columns(t, dz, dc):
        there_z, there_c = at(dz, dc)
        ref, _, _, cols = weights[t]
        first = pl.multiple_of((lax.rem(there_z, 2) * 2 + there_c) * cols, cols)
        return ref.at[:, pl.ds(first, cols)]

    def send(t, i):
        return remote(
            columns(t, *rels[i]), slot(t, 0, 0, x), w_send.at[t, i], w_recv.at[t, i], device(*rels[i])
        )

    def arrived(t, i):
        here = slot(t, *rels[i], x)
        return remote(here, here, w_send.at[t, i], w_recv.at[t, i], device(*rels[i]))

    def forward(t, i):
        here = slot(t, *rels[i], x)
        source = columns(t, 0, 0) if i == 0 else here
        return remote(source, here, f_send.at[t, i], f_recv.at[t, i], x_mate)

    def forwarded(t, i):
        here = slot(t, *rels[i], 1 - x)
        return remote(here, here, f_send.at[t, i], f_recv.at[t, i], x_mate)

    chunks = x_ref.shape[0]

    def x_slot(row, core, half):
        return x_all.at[pl.ds(half * chunks, chunks), row * 2 + core]

    def x_copy(i, source, row, half, to):
        return remote(source, x_slot(row, c, half), x_send.at[i], x_recv.at[i], to)

    def x_arrived(i, row, core, half):
        here = x_slot(row, core, half)
        return remote(here, here, x_send.at[i], x_recv.at[i], z_mate)

    def own(t):
        return pltpu.make_async_copy(columns(t, 0, 0), slot(t, 0, 0, x), local_sem.at[t])

    own_x = pltpu.make_async_copy(x_ref, x_slot(zz, c, y), local_sem.at[4])
    x_copies = [
        x_copy(0, x_ref, zz, y, z_mate),
        x_copy(1, x_ref, zz, y, y_mate),
        x_copy(2, x_ref, zz, y, c_mate),
    ]
    for copy in x_copies:
        copy.start()
    own_x.start()
    for t in (0, 1, 2, 3):
        own(t).start()

    order = [1] + list(range(4, 6)) + list(range(2, 4)) + list(range(6, len(rels)))
    items = [(t, i) for t in range(4) for i in order]
    window = len(order) + 1

    def start_item(n):
        if n < len(items):
            send(*items[n]).start()
            if items[n][1] == order[0]:
                forward(items[n][0], 0).start()

    def roll(first, last):
        for n in range(first, last):
            arrived(*items[n]).wait_recv()
            start_item(n + window)
            forward(*items[n]).start()

    for n in range(window):
        start_item(n)
    roll(0, 2)
    x_arrived(0, 1 - zz, c, y).wait_recv()
    x_copies.append(x_copy(3, x_slot(1 - zz, c, y), 1 - zz, y, y_mate))
    x_copies.append(x_copy(4, x_slot(1 - zz, c, y), 1 - zz, y, c_mate))
    for copy in x_copies[3:]:
        copy.start()
    roll(2, 7)
    x_arrived(1, zz, c, 1 - y).wait_recv()
    x_copies.append(x_copy(5, x_slot(zz, c, 1 - y), zz, 1 - y, c_mate))
    x_copies[5].start()
    per = len(order)
    roll(7, 2 * per)
    x_arrived(3, 1 - zz, c, 1 - y).wait_recv()
    x_copies.append(x_copy(6, x_slot(1 - zz, c, 1 - y), 1 - zz, 1 - y, c_mate))
    x_copies[6].start()
    roll(2 * per, 3 * per)

    x_arrived(2, zz, 1 - c, y).wait_recv()
    x_arrived(4, 1 - zz, 1 - c, y).wait_recv()
    x_arrived(5, zz, 1 - c, 1 - y).wait_recv()
    x_arrived(6, 1 - zz, 1 - c, 1 - y).wait_recv()
    own_x.wait()

    def multiply(weight, out_ref):
        blocks, tok = x_all.shape[1], x_all.shape[2]
        out_ref[...] = jnp.zeros_like(out_ref)

        def one(step, carry):
            j, k = step // blocks, step % blocks
            rows = pl.ds(pl.multiple_of(k * tok, tok), tok)
            out_ref[rows, :] += jnp.dot(
                x_all[j, k], weight[j], preferred_element_type=jnp.float32
            )
            return carry

        lax.fori_loop(0, x_all.shape[0] * blocks, one, 0)

    for t in (0, 1):
        own(t).wait()
        for i in range(len(rels)):
            forwarded(t, i).wait_recv()
    multiply(kv_all, kv_ref)
    roll(3 * per, 4 * per)
    own(2).wait()
    for i in range(len(rels)):
        forwarded(2, i).wait_recv()
    multiply(q_all, q_ref)
    own(3).wait()
    for i in range(len(rels)):
        forwarded(3, i).wait_recv()
    for copy in x_copies:
        copy.wait_send()
    for t in range(4):
        for i in range(len(rels)):
            if i > 0:
                send(t, i).wait_send()
            forward(t, i).wait_send()


def gathered_products(normed, key_weight, value_weight, w_query, w_out):
    tok, half_width = normed.shape
    rows = key_weight.shape[0]
    planes = lax.axis_size("z")
    kv_cols, q_cols = key_weight.shape[1] // 2, w_query.shape[1] // 4
    places = planes * 4
    chunks = half_width // rows
    split = jnp.transpose(normed.reshape(tok, chunks, rows), (1, 0, 2))
    any_space = pl.BlockSpec(memory_space=pl.ANY)
    vmem_space = pl.BlockSpec(memory_space=pltpu.VMEM)
    dma = pltpu.SemaphoreType.DMA
    kv_raw, q_raw, o_all = pl.pallas_call(
        functools.partial(gather_kernel, planes),
        out_shape=(
            jax.ShapeDtypeStruct((4 * tok, kv_cols), jnp.float32),
            jax.ShapeDtypeStruct((4 * tok, q_cols), jnp.float32),
            jax.ShapeDtypeStruct((places, rows, q_cols), jnp.bfloat16),
        ),
        in_specs=[any_space] * 5,
        out_specs=(vmem_space, vmem_space, any_space),
        scratch_shapes=[
            pltpu.VMEM((places, 4, tok, rows), jnp.bfloat16),
            pltpu.VMEM((places, rows, kv_cols), jnp.bfloat16),
            pltpu.VMEM((places, rows, q_cols), jnp.bfloat16),
            dma((7,)),
            dma((7,)),
            dma((4, places // 2)),
            dma((4, places // 2)),
            dma((4, places // 2)),
            dma((4, places // 2)),
            dma((5,)),
        ],
        compiler_params=pltpu.CompilerParams(
            collective_id=0, has_side_effects=True, vmem_limit_bytes=44 << 20
        ),
    )(split, key_weight, value_weight, w_query, w_out)
    return kv_raw, q_raw, o_all.reshape(places * rows, q_cols)


def rearranged(
    residual,
    input_gain,
    w_query,
    key_weight,
    value_weight,
    query_gain,
    key_gain,
    w_out,
    post_gain,
    positions,
):
    tok, half_width = residual.shape
    head_dim = query_gain.shape[0]
    z, x, c = lax.axis_index("z"), lax.axis_index("x"), lax.axis_index("c")
    y = lax.axis_index("y")
    pair, zz = z // 2, z % 2
    kv_cols = key_weight.shape[1] // 4
    q_cols = w_query.shape[1] // 4
    kv_heads = kv_cols // head_dim
    group = q_cols // kv_cols
    run = 2 * tok
    full_width = 2 * half_width

    stream = residual.astype(jnp.float32)
    squares = jnp.sum(stream * stream, axis=1, keepdims=True)
    squares = squares + swap(squares, "y")
    gain_in = lax.dynamic_slice_in_dim(input_gain, y * half_width, half_width, 0)
    normed = (stream * lax.rsqrt(squares / full_width + epsilon) * gain_in).astype(jnp.bfloat16)
    kv_raw, q_raw, o_all = gathered_products(
        normed, key_weight, value_weight, w_query, w_out.T
    )

    def places_of(i):
        return lax.dynamic_slice_in_dim(positions, (4 * pair + 2 * i + x) * run, run, 0)

    places = jnp.concatenate([places_of(0), places_of(1)])
    keys = rotary(
        norm_scale(kv_raw[:, :kv_cols].reshape(2 * run, kv_heads, head_dim), key_gain), places
    ).reshape(2 * run, kv_cols)
    kv = jnp.concatenate([keys, kv_raw[:, kv_cols:]], axis=1).astype(jnp.bfloat16)
    kv = kv.reshape(2, run, 2 * kv_cols)
    before = from_behind(kv[1], "z", 2)
    own = jnp.concatenate([before[None], kv])
    across = jnp.concatenate([swap(before, "x")[None], swap(kv, "x")])
    kv_runs = in_order(x, own, across, axis=1).reshape(6 * run, 2 * kv_cols)
    key_places = lax.dynamic_slice_in_dim(
        jnp.concatenate([jnp.zeros((2 * run,), jnp.int32), positions]), 4 * pair * run, 6 * run, 0
    )
    key_index = (4 * pair - 2) * run + jnp.arange(6 * run, dtype=jnp.int32)
    key_places = jnp.where(key_index >= 0, key_places, jnp.int32(1 << 30))

    queries = rotary(
        norm_scale(q_raw.reshape(2 * run, kv_heads * group, head_dim), query_gain), places
    ).astype(jnp.bfloat16)
    queries = queries.reshape(2, run, kv_heads, group, head_dim)

    def attend(i):
        start = (2 * i + x) * run
        window = lax.dynamic_slice_in_dim(kv_runs, start, 3 * run, 0)
        window_places = lax.dynamic_slice_in_dim(key_places, start, 3 * run, 0)
        window_keys = window[:, :kv_cols].reshape(3 * run, kv_heads, head_dim)
        window_values = window[:, kv_cols:].reshape(3 * run, kv_heads, head_dim)
        scores = (
            jnp.einsum(
                "qkgd,skd->kgqs", queries[i], window_keys, preferred_element_type=jnp.float32
            )
            * score_scale
        )
        distance = places_of(i)[:, None] - window_places[None, :]
        allowed = (distance >= 0) & (distance < LOOKBACK_SPAN)
        weights = jnp.where(allowed[None, None], jnp.exp(scores), jnp.zeros_like(scores))
        total = jnp.sum(weights, axis=-1)
        summed = jnp.einsum(
            "kgqs,skd->qkgd",
            weights.astype(jnp.bfloat16),
            window_values,
            preferred_element_type=jnp.float32,
        )
        merged = summed / jnp.transpose(total, (2, 0, 1))[..., None]
        return merged.astype(jnp.bfloat16).reshape(run, q_cols)

    attended = jnp.stack([attend(0), attend(1)]).reshape(2, 2, tok, q_cols)

    def project(block):
        return lax.dot_general(
            block, o_all, (((1,), (1,)), ((), ())), preferred_element_type=jnp.float32
        )

    def exchange(block, axis):
        return swap(block.astype(jnp.bfloat16), axis).astype(jnp.float32)

    def core_sum(block):
        return exchange(project(pick(block, 1 - c, 0)), "c") + project(pick(block, c, 0))

    half_tok = tok // 2
    away = core_sum(pick(attended, 1 - zz, 0))
    home = core_sum(pick(attended, zz, 0))
    first = exchange(away[:half_tok], "z")
    away_cross = exchange(away[half_tok:, half_width:], "y")
    home_cross = exchange(home[half_tok:, half_width:], "y")
    upper = home[:half_tok] + first
    lower = away[half_tok:, :half_width] + away_cross
    upper_sum = upper[:, :half_width] + exchange(upper[:, half_width:], "y")
    lower_sum = home[half_tok:, :half_width] + home_cross + exchange(lower, "z")
    attn_sum = jnp.concatenate([upper_sum, lower_sum], axis=0)
    squares = jnp.sum(attn_sum * attn_sum, axis=1, keepdims=True)
    squares = squares + swap(squares, "y")
    gain_out = lax.dynamic_slice_in_dim(post_gain, y * half_width, half_width, 0)
    return (stream + attn_sum * lax.rsqrt(squares / full_width + epsilon) * gain_out).astype(
        jnp.bfloat16
    )


def solution(mesh):
    seq, tp = mesh.shape["seq"], mesh.shape["tp"]
    if tp == 2 and seq % 16 == 0:
        mesh = Mesh(mesh.devices.reshape(seq // 4, 2, 2, tp), ("z", "x", "c", "y"))
        seq_axes, tp_axes, body = ("z", "x", "c"), "y", rearranged
    else:
        seq_axes, tp_axes, body = "seq", "tp", local
    in_specs = (
        P(seq_axes, tp_axes),
        P(),
        P(seq_axes, tp_axes),
        P(seq_axes, tp_axes),
        P(seq_axes, tp_axes),
        P(),
        P(),
        P(tp_axes, seq_axes),
        P(),
        P(),
    )
    out_specs = P(seq_axes, tp_axes)
    return jax.shard_map(body, mesh=mesh, in_specs=in_specs, out_specs=out_specs, check_vma=False)
```

```python
import functools

import jax
import jax.numpy as jnp
from jax import lax
from jax.experimental import pallas as pl
from jax.experimental.pallas import tpu as pltpu
from jax.sharding import Mesh
from jax.sharding import PartitionSpec as P

LOOKBACK_SPAN = 1024


epsilon = 1e-06
score_scale = 168.0 ** (-0.5)
rotary_base = 10000.0


def from_behind(block, axis, distance):
    devices = range(lax.axis_size(axis))
    route = [(i - distance, i) for i in devices if i - distance in devices]
    return lax.ppermute(block, axis, route)


def norm_scale(value_matrix, gain):
    mean_square = jnp.mean(value_matrix * value_matrix, axis=-1, keepdims=True)
    return value_matrix * lax.rsqrt(mean_square + epsilon) * gain


def rotary(value_matrix, places):
    half_dim = value_matrix.shape[-1] // 2
    inverse = rotary_base ** (-jnp.arange(half_dim, dtype=jnp.float32) / half_dim)
    angles = places.astype(jnp.float32)[:, None] * inverse[None, :]
    cosine = jnp.cos(angles)[:, None, :]
    sine = jnp.sin(angles)[:, None, :]
    first = value_matrix[..., :half_dim]
    second = value_matrix[..., half_dim:]
    return jnp.concatenate(
        [first * cosine - second * sine, second * cosine + first * sine], axis=-1
    )


def local(
    residual,
    input_gain,
    w_query,
    key_weight,
    value_weight,
    query_gain,
    key_gain,
    w_out,
    post_gain,
    positions,
):
    tok_rows = residual.shape[0]
    seq_at = lax.axis_index("seq")
    tp_at = lax.axis_index("tp")
    head_dim = query_gain.shape[0]
    local_kv = key_weight.shape[1] // head_dim
    query_group = w_query.shape[1] // key_weight.shape[1]
    gathered = lax.all_gather(residual, "tp", axis=1, tiled=True)
    normalized_input = norm_scale(gathered.astype(jnp.float32), input_gain).astype(jnp.bfloat16)
    own_places = lax.dynamic_slice_in_dim(positions, seq_at * tok_rows, tok_rows, 0)
    reach = (LOOKBACK_SPAN - 2) // tok_rows + 1

    def attend(query_matrix, stacked, key_places, valid):
        key_matrix = stacked[0].reshape(-1, local_kv, head_dim)
        value_matrix = stacked[1].reshape(-1, local_kv, head_dim)
        scores = (
            jnp.einsum(
                "qkgd,skd->kgqs", query_matrix, key_matrix, preferred_element_type=jnp.float32
            )
            * score_scale
        )
        distance = own_places[:, None] - key_places[None, :]
        allowed = valid[None, :] & (distance >= 0) & (distance < LOOKBACK_SPAN)
        weights = jnp.where(allowed[None, None], jnp.exp(scores), jnp.zeros_like(scores))
        total = jnp.sum(weights, axis=-1)
        summed = jnp.einsum(
            "kgqs,skd->qkgd",
            weights.astype(jnp.bfloat16),
            value_matrix,
            preferred_element_type=jnp.float32,
        )
        return (total, summed)

    pieces = (
        lax.all_gather(w_query, "seq", axis=0, tiled=True),
        lax.all_gather(key_weight, "seq", axis=0, tiled=True),
        lax.all_gather(value_weight, "seq", axis=0, tiled=True),
    )
    queries_raw, unrotated_keys, projected_values = tuple(
        (jnp.dot(normalized_input, piece, preferred_element_type=jnp.float32) for piece in pieces)
    )
    key_matrix = rotary(
        norm_scale(unrotated_keys.reshape(tok_rows, local_kv, head_dim), key_gain), own_places
    )
    stacked = jnp.stack(
        [key_matrix.reshape(tok_rows, local_kv * head_dim), projected_values]
    ).astype(jnp.bfloat16)
    pieces = []
    for distance in range(reach, 0, -1):
        pieces.append(from_behind(stacked, "seq", distance))
    halo = jnp.concatenate(pieces, axis=1)
    query_matrix = rotary(
        norm_scale(queries_raw.reshape(tok_rows, local_kv * query_group, head_dim), query_gain),
        own_places,
    )
    query_matrix = query_matrix.astype(jnp.bfloat16).reshape(
        tok_rows, local_kv, query_group, head_dim
    )
    inner_total, inner_sum = attend(
        query_matrix, stacked, own_places, jnp.ones((tok_rows,), jnp.bool_)
    )
    span = halo.shape[1]
    padded_places = jnp.concatenate([jnp.zeros((span,), jnp.int32), positions])
    halo_places = lax.dynamic_slice_in_dim(padded_places, seq_at * tok_rows, span, 0)
    halo_valid = seq_at * tok_rows - span + jnp.arange(span, dtype=jnp.int32) >= 0
    outer_total, outer_sum = attend(query_matrix, halo, halo_places, halo_valid)
    total = jnp.transpose(inner_total + outer_total, (2, 0, 1))
    merged = (inner_sum + outer_sum) / total[..., None]
    attended = merged.astype(jnp.bfloat16).reshape(tok_rows, local_kv * query_group * head_dim)
    partial_out = jnp.dot(
        attended,
        lax.all_gather(w_out, "seq", axis=1, tiled=True),
        preferred_element_type=jnp.float32,
    )
    summed_cols = lax.psum_scatter(
        partial_out.astype(jnp.bfloat16), "tp", scatter_dimension=1, tiled=True
    ).astype(jnp.float32)
    full_width = post_gain.shape[0]
    squares = lax.psum(jnp.sum(summed_cols * summed_cols, axis=1), "tp")
    inverse_rms = lax.rsqrt(squares / full_width + epsilon)
    gain_part = lax.dynamic_slice_in_dim(
        post_gain, tp_at * summed_cols.shape[1], summed_cols.shape[1], 0
    )
    return (residual.astype(jnp.float32) + summed_cols * inverse_rms[:, None] * gain_part).astype(
        jnp.bfloat16
    )


def swap(block, axis):
    size = lax.axis_size(axis)
    return lax.ppermute(block, axis, [(i, i ^ 1) for i in range(size)])


def shift(block, axis, distance):
    size = lax.axis_size(axis)
    return lax.ppermute(block, axis, [(i, (i + distance) % size) for i in range(size)])


def pick(block, index, axis):
    return lax.dynamic_index_in_dim(block, index, axis, keepdims=False)


def in_order(at, own, other, axis=0):
    return jnp.stack(
        [jnp.where(at == 0, own, other), jnp.where(at == 0, other, own)], axis=axis
    )


def gather_kernel(
    planes,
    x_ref,
    wk_ref,
    wv_ref,
    wq_ref,
    wo_ref,
    kv_ref,
    q_ref,
    o_ref,
    x_all,
    kv_all,
    q_all,
    x_send,
    x_recv,
    w_send,
    w_recv,
    f_send,
    f_recv,
    local_sem,
):
    z, x, c = lax.axis_index("z"), lax.axis_index("x"), lax.axis_index("c")
    y = lax.axis_index("y")
    zz = lax.rem(z, 2)
    rels = [(dz, dc) for dz in range(planes) for dc in range(2)]

    def at(dz, dc):
        return lax.rem(z + dz + planes, planes), lax.rem(c + dc + 2, 2)

    def device(dz, dc):
        there_z, there_c = at(dz, dc)
        return (there_z, x, there_c, y)

    x_mate = (z, 1 - x, c, y)
    y_mate = (z, x, c, 1 - y)
    c_mate = (z, x, 1 - c, y)
    z_mate = (z + 1 - 2 * zz, x, c, y)

    barrier = pltpu.get_barrier_semaphore()
    peers = [device(*rel) for rel in rels[1:]] + [x_mate, y_mate]
    for peer in peers:
        pl.semaphore_signal(barrier, inc=1, device_id=peer, device_id_type=pl.DeviceIdType.MESH)
    pl.semaphore_wait(barrier, len(peers))

    def remote(src, dst, send, recv, to):
        return pltpu.make_async_remote_copy(
            src_ref=src,
            dst_ref=dst,
            send_sem=send,
            recv_sem=recv,
            device_id=to,
            device_id_type=pl.DeviceIdType.MESH,
        )

    kv_cols = wk_ref.shape[1] // 4
    q_cols = wq_ref.shape[1] // 4
    weights = (
        (wk_ref, kv_all, 0, kv_cols),
        (wv_ref, kv_all, kv_cols, kv_cols),
        (wq_ref, q_all, 0, q_cols),
        (wo_ref, o_ref, 0, q_cols),
    )

    def slot(t, dz, dc, side):
        there_z, there_c = at(-dz, -dc)
        _, buf, low, cols = weights[t]
        if t == 3:
            there_z = lax.rem(there_z + y * (planes // 2), planes)
        return buf.at[(there_z * 2 + side) * 2 + there_c, :, pl.ds(low, cols)]

    def columns(t, dz, dc):
        there_z, there_c = at(dz, dc)
        ref, _, _, cols = weights[t]
        first = pl.multiple_of((lax.rem(there_z, 2) * 2 + there_c) * cols, cols)
        return ref.at[:, pl.ds(first, cols)]

    def send(t, i):
        return remote(
            columns(t, *rels[i]), slot(t, 0, 0, x), w_send.at[t, i], w_recv.at[t, i], device(*rels[i])
        )

    def arrived(t, i):
        here = slot(t, *rels[i], x)
        return remote(here, here, w_send.at[t, i], w_recv.at[t, i], device(*rels[i]))

    def forward(t, i):
        here = slot(t, *rels[i], x)
        source = columns(t, 0, 0) if i == 0 else here
        return remote(source, here, f_send.at[t, i], f_recv.at[t, i], x_mate)

    def forwarded(t, i):
        here = slot(t, *rels[i], 1 - x)
        return remote(here, here, f_send.at[t, i], f_recv.at[t, i], x_mate)

    chunks = x_ref.shape[0]

    def x_slot(row, core, half):
        return x_all.at[pl.ds(half * chunks, chunks), row * 2 + core]

    def x_copy(i, source, row, half, to):
        return remote(source, x_slot(row, c, half), x_send.at[i], x_recv.at[i], to)

    def x_arrived(i, row, core, half):
        here = x_slot(row, core, half)
        return remote(here, here, x_send.at[i], x_recv.at[i], z_mate)

    def own(t):
        return pltpu.make_async_copy(columns(t, 0, 0), slot(t, 0, 0, x), local_sem.at[t])

    own_x = pltpu.make_async_copy(x_ref, x_slot(zz, c, y), local_sem.at[4])
    x_copies = [
        x_copy(0, x_ref, zz, y, z_mate),
        x_copy(1, x_ref, zz, y, y_mate),
        x_copy(2, x_ref, zz, y, c_mate),
    ]
    for copy in x_copies:
        copy.start()
    own_x.start()
    for t in (0, 1, 2, 3):
        own(t).start()

    order = [1] + list(range(4, 6)) + list(range(2, 4)) + list(range(6, len(rels)))
    items = [(t, i) for t in range(4) for i in order]
    window = len(order) - 2

    def start_item(n):
        if n < len(items):
            send(*items[n]).start()
            if items[n][1] == order[0]:
                forward(items[n][0], 0).start()

    def roll(first, last):
        for n in range(first, last):
            arrived(*items[n]).wait_recv()
            start_item(n + window)
            forward(*items[n]).start()

    for n in range(window):
        start_item(n)
    roll(0, 2)
    x_arrived(0, 1 - zz, c, y).wait_recv()
    x_copies.append(x_copy(3, x_slot(1 - zz, c, y), 1 - zz, y, y_mate))
    x_copies.append(x_copy(4, x_slot(1 - zz, c, y), 1 - zz, y, c_mate))
    for copy in x_copies[3:]:
        copy.start()
    roll(2, 7)
    x_arrived(1, zz, c, 1 - y).wait_recv()
    x_copies.append(x_copy(5, x_slot(zz, c, 1 - y), zz, 1 - y, c_mate))
    x_copies[5].start()
    per = len(order)
    roll(7, 2 * per)
    x_arrived(3, 1 - zz, c, 1 - y).wait_recv()
    x_copies.append(x_copy(6, x_slot(1 - zz, c, 1 - y), 1 - zz, 1 - y, c_mate))
    x_copies[6].start()
    roll(2 * per, 3 * per)

    x_arrived(2, zz, 1 - c, y).wait_recv()
    x_arrived(4, 1 - zz, 1 - c, y).wait_recv()
    x_arrived(5, zz, 1 - c, 1 - y).wait_recv()
    x_arrived(6, 1 - zz, 1 - c, 1 - y).wait_recv()
    own_x.wait()

    def multiply(weight, out_ref):
        blocks, tok = x_all.shape[1], x_all.shape[2]
        out_ref[...] = jnp.zeros_like(out_ref)

        def one(step, carry):
            j, k = step // blocks, step % blocks
            rows = pl.ds(pl.multiple_of(k * tok, tok), tok)
            out_ref[rows, :] += jnp.dot(
                x_all[j, k], weight[j], preferred_element_type=jnp.float32
            )
            return carry

        lax.fori_loop(0, x_all.shape[0] * blocks, one, 0)

    for t in (0, 1):
        own(t).wait()
        for i in range(len(rels)):
            forwarded(t, i).wait_recv()
    multiply(kv_all, kv_ref)
    roll(3 * per, 4 * per)
    own(2).wait()
    for i in range(len(rels)):
        forwarded(2, i).wait_recv()
    multiply(q_all, q_ref)
    own(3).wait()
    for i in range(len(rels)):
        forwarded(3, i).wait_recv()
    for copy in x_copies:
        copy.wait_send()
    for t in range(4):
        for i in range(len(rels)):
            if i > 0:
                send(t, i).wait_send()
            forward(t, i).wait_send()


def gathered_products(normed, key_weight, value_weight, w_query, w_out):
    tok, half_width = normed.shape
    rows = key_weight.shape[0]
    planes = lax.axis_size("z")
    kv_cols, q_cols = key_weight.shape[1] // 2, w_query.shape[1] // 4
    places = planes * 4
    chunks = half_width // rows
    split = jnp.transpose(normed.reshape(tok, chunks, rows), (1, 0, 2))
    any_space = pl.BlockSpec(memory_space=pl.ANY)
    vmem_space = pl.BlockSpec(memory_space=pltpu.VMEM)
    dma = pltpu.SemaphoreType.DMA
    kv_raw, q_raw, o_all = pl.pallas_call(
        functools.partial(gather_kernel, planes),
        out_shape=(
            jax.ShapeDtypeStruct((4 * tok, kv_cols), jnp.float32),
            jax.ShapeDtypeStruct((4 * tok, q_cols), jnp.float32),
            jax.ShapeDtypeStruct((places, rows, q_cols), jnp.bfloat16),
        ),
        in_specs=[any_space] * 5,
        out_specs=(vmem_space, vmem_space, any_space),
        scratch_shapes=[
            pltpu.VMEM((places, 4, tok, rows), jnp.bfloat16),
            pltpu.VMEM((places, rows, kv_cols), jnp.bfloat16),
            pltpu.VMEM((places, rows, q_cols), jnp.bfloat16),
            dma((7,)),
            dma((7,)),
            dma((4, places // 2)),
            dma((4, places // 2)),
            dma((4, places // 2)),
            dma((4, places // 2)),
            dma((5,)),
        ],
        compiler_params=pltpu.CompilerParams(
            collective_id=0, has_side_effects=True, vmem_limit_bytes=44 << 20
        ),
    )(split, key_weight, value_weight, w_query, w_out)
    return kv_raw, q_raw, o_all.reshape(places * rows, q_cols)


def rearranged(
    residual,
    input_gain,
    w_query,
    key_weight,
    value_weight,
    query_gain,
    key_gain,
    w_out,
    post_gain,
    positions,
):
    tok, half_width = residual.shape
    head_dim = query_gain.shape[0]
    z, x, c = lax.axis_index("z"), lax.axis_index("x"), lax.axis_index("c")
    y = lax.axis_index("y")
    pair, zz = z // 2, z % 2
    kv_cols = key_weight.shape[1] // 4
    q_cols = w_query.shape[1] // 4
    kv_heads = kv_cols // head_dim
    group = q_cols // kv_cols
    run = 2 * tok
    full_width = 2 * half_width

    stream = residual.astype(jnp.float32)
    squares = jnp.sum(stream * stream, axis=1, keepdims=True)
    squares = squares + swap(squares, "y")
    gain_in = lax.dynamic_slice_in_dim(input_gain, y * half_width, half_width, 0)
    normed = (stream * lax.rsqrt(squares / full_width + epsilon) * gain_in).astype(jnp.bfloat16)
    kv_raw, q_raw, o_all = gathered_products(
        normed, key_weight, value_weight, w_query, w_out.T
    )

    def places_of(i):
        return lax.dynamic_slice_in_dim(positions, (4 * pair + 2 * i + x) * run, run, 0)

    places = jnp.concatenate([places_of(0), places_of(1)])
    keys = rotary(
        norm_scale(kv_raw[:, :kv_cols].reshape(2 * run, kv_heads, head_dim), key_gain), places
    ).reshape(2 * run, kv_cols)
    kv = jnp.concatenate([keys, kv_raw[:, kv_cols:]], axis=1).astype(jnp.bfloat16)
    kv = kv.reshape(2, run, 2 * kv_cols)
    before = from_behind(kv[1], "z", 2)
    own = jnp.concatenate([before[None], kv])
    across = jnp.concatenate([swap(before, "x")[None], swap(kv, "x")])
    kv_runs = in_order(x, own, across, axis=1).reshape(6 * run, 2 * kv_cols)
    key_places = lax.dynamic_slice_in_dim(
        jnp.concatenate([jnp.zeros((2 * run,), jnp.int32), positions]), 4 * pair * run, 6 * run, 0
    )
    key_index = (4 * pair - 2) * run + jnp.arange(6 * run, dtype=jnp.int32)
    key_places = jnp.where(key_index >= 0, key_places, jnp.int32(1 << 30))

    queries = rotary(
        norm_scale(q_raw.reshape(2 * run, kv_heads * group, head_dim), query_gain), places
    ).astype(jnp.bfloat16)
    queries = queries.reshape(2, run, kv_heads, group, head_dim)

    def attend(i):
        start = (2 * i + x) * run
        window = lax.dynamic_slice_in_dim(kv_runs, start, 3 * run, 0)
        window_places = lax.dynamic_slice_in_dim(key_places, start, 3 * run, 0)
        window_keys = window[:, :kv_cols].reshape(3 * run, kv_heads, head_dim)
        window_values = window[:, kv_cols:].reshape(3 * run, kv_heads, head_dim)
        scores = (
            jnp.einsum(
                "qkgd,skd->kgqs", queries[i], window_keys, preferred_element_type=jnp.float32
            )
            * score_scale
        )
        distance = places_of(i)[:, None] - window_places[None, :]
        allowed = (distance >= 0) & (distance < LOOKBACK_SPAN)
        weights = jnp.where(allowed[None, None], jnp.exp(scores), jnp.zeros_like(scores))
        total = jnp.sum(weights, axis=-1)
        summed = jnp.einsum(
            "kgqs,skd->qkgd",
            weights.astype(jnp.bfloat16),
            window_values,
            preferred_element_type=jnp.float32,
        )
        merged = summed / jnp.transpose(total, (2, 0, 1))[..., None]
        return merged.astype(jnp.bfloat16).reshape(run, q_cols)

    attended = jnp.stack([attend(0), attend(1)]).reshape(2, 2, tok, q_cols)

    def project(block):
        return lax.dot_general(
            block, o_all, (((1,), (1,)), ((), ())), preferred_element_type=jnp.float32
        )

    def exchange(block, axis):
        return swap(block.astype(jnp.bfloat16), axis).astype(jnp.float32)

    def core_sum(block):
        return exchange(project(pick(block, 1 - c, 0)), "c") + project(pick(block, c, 0))

    half_tok = tok // 2
    away = core_sum(pick(attended, 1 - zz, 0))
    home = core_sum(pick(attended, zz, 0))
    first = exchange(away[:half_tok], "z")
    away_cross = exchange(away[half_tok:, half_width:], "y")
    home_cross = exchange(home[half_tok:, half_width:], "y")
    upper = home[:half_tok] + first
    lower = away[half_tok:, :half_width] + away_cross
    upper_sum = upper[:, :half_width] + exchange(upper[:, half_width:], "y")
    lower_sum = home[half_tok:, :half_width] + home_cross + exchange(lower, "z")
    attn_sum = jnp.concatenate([upper_sum, lower_sum], axis=0)
    squares = jnp.sum(attn_sum * attn_sum, axis=1, keepdims=True)
    squares = squares + swap(squares, "y")
    gain_out = lax.dynamic_slice_in_dim(post_gain, y * half_width, half_width, 0)
    return (stream + attn_sum * lax.rsqrt(squares / full_width + epsilon) * gain_out).astype(
        jnp.bfloat16
    )


def solution(mesh):
    seq, tp = mesh.shape["seq"], mesh.shape["tp"]
    if tp == 2 and seq % 16 == 0:
        mesh = Mesh(mesh.devices.reshape(seq // 4, 2, 2, tp), ("z", "x", "c", "y"))
        seq_axes, tp_axes, body = ("z", "x", "c"), "y", rearranged
    else:
        seq_axes, tp_axes, body = "seq", "tp", local
    in_specs = (
        P(seq_axes, tp_axes),
        P(),
        P(seq_axes, tp_axes),
        P(seq_axes, tp_axes),
        P(seq_axes, tp_axes),
        P(),
        P(),
        P(tp_axes, seq_axes),
        P(),
        P(),
    )
    out_specs = P(seq_axes, tp_axes)
    return jax.shard_map(body, mesh=mesh, in_specs=in_specs, out_specs=out_specs, check_vma=False)
```
